256 devices in a mesh: seq: 128 (over y, x, z_hi, core), head: 2 (over z_lo).
Axes of the slice: x: 4, y: 4, z: 8 (z_hi: 4, z_lo: 2; z = z_hi * 2 + z_lo), core: 2. Of those that a mesh axis runs over, the one named last changes fastest.
Arguments:
- video: bfloat16 [30720, 3072], P('seq'), may hold values from -26 to 26
- audio: bfloat16 [128, 3072], P(None, 'seq'), may hold values from -26 to 26
- video_gain: float32 [3072], replicated, may hold values from 0.5 to 2
- audio_gain: float32 [3072], P('seq'), may hold values from 0.5 to 2
- wq_video: bfloat16 [3072, 1536], P('seq', 'head'), may hold values from -1 to 1
- wk_video: bfloat16 [3072, 1536], P('seq', 'head'), may hold values from -1 to 1
- wv_video: bfloat16 [3072, 1536], P('seq', 'head'), may hold values from -0.109375 to 0.109375
- wq_audio: bfloat16 [3072, 1536], P('seq', 'head'), may hold values from -1 to 1
- wk_audio: bfloat16 [3072, 1536], P('seq', 'head'), may hold values from -1 to 1
- wv_audio: bfloat16 [3072, 1536], P('seq', 'head'), may hold values from -0.109375 to 0.109375
Outputs:
- video_mix: bfloat16 [30720, 1536], P('seq', 'head')
- audio_mix: bfloat16 [128, 1536], P('seq', 'head')
The draws below stay inside these ranges and needn't reach their ends.
All inputs are finite; a program needn't handle non-finite values.
Results may differ from the reference program's by a relative error of at most 0.012.
Values may be sent and summed in bfloat16 or wider, within the bound.
No kernel may reach another device: no remote copies, remote signals or barrier semaphores. Data moves between devices by JAX's collectives and lax.ppermute only.
A program may use at most 128 MiB of HBM per device.

```python
import math
import jax
import jax.numpy as jnp
from jax import lax

D = 3072
HEADS = 12
HD = 128
TOK_DEV = 240
NV = 30720
NA = 128
N_SEQ = 128


def weight_rows(key):
    base = jnp.clip(jax.random.normal(key, (D, HEADS * HD), jnp.float32), -4.0, 4.0) * (1.0 / math.sqrt(D))
    return base.astype(jnp.bfloat16)


def token_rows(key, rows):
    first = jax.random.fold_in(key, 0)
    base = jnp.clip(jax.random.normal(first, (rows, D), jnp.float32), -6.0, 6.0)
    return base.astype(jnp.bfloat16)


def draw_video(key, part):
    key = jax.random.fold_in(key, 21)
    return token_rows(key, NV)


def draw_audio(key, part):
    key = jax.random.fold_in(key, 22)
    return token_rows(key, NA)


def draw_wq_video(key, part):
    key = jax.random.fold_in(key, 31)
    return weight_rows(key)


def draw_wk_video(key, part):
    key = jax.random.fold_in(key, 32)
    return weight_rows(key)


def draw_wq_audio(key, part):
    key = jax.random.fold_in(key, 33)
    return weight_rows(key)


def draw_wk_audio(key, part):
    key = jax.random.fold_in(key, 34)
    return weight_rows(key)


def block_levels(rng, dims, cuts, least, largest):
    def one(axis_at, parts):
        draws = jax.random.uniform(jax.random.fold_in(jax.random.fold_in(rng, 6), axis_at), (parts,), jnp.float32, least / len(cuts), largest / len(cuts))
        return jnp.repeat(jnp.exp(draws), dims[axis_at] // parts).reshape((-1,) + (1,) * (len(dims) - axis_at - 1))

    factor_of = one(*cuts[0])
    for cut in cuts[1:]:
        factor_of = factor_of * one(*cut)
    return factor_of


def centred(key, extent, width, bound, pieces=(), dtype=jnp.bfloat16):
    level = block_levels(key, extent, pieces, -0.22, 0.18) if pieces else 1.0
    values = jax.random.normal(key, extent, jnp.float32) * width * level
    return jnp.minimum(jnp.maximum(values, -bound), bound).astype(dtype)


def setup_inputs(seed: int = 0) -> dict:
    key_list = jax.random.split(jax.random.key(seed), 11)
    video = draw_video(jax.random.fold_in(key_list[10], 71), 0)
    audio = draw_audio(jax.random.fold_in(key_list[10], 71), 0)
    video_gain = jnp.clip(jnp.exp(jax.random.uniform(key_list[2], (D,), jnp.float32, math.log(0.5), math.log(2.0))), 0.5, 2.0)
    audio_gain = jnp.clip(jnp.exp(math.log(2.0) - 1.3862944 * jax.random.uniform(key_list[3], (D,), jnp.float32) ** block_levels(key_list[3], (D,), ((0, 128),), -0.2, 0.2)), 0.5, 2.0)
    wq_video = draw_wq_video(jax.random.fold_in(key_list[10], 71), 0)
    wk_video = draw_wk_video(jax.random.fold_in(key_list[10], 71), 0)
    wv_video = centred(key_list[6], (D, HEADS * HD), D ** -0.5, 0.109375, ((0, 128), (1, 2)))
    wq_audio = draw_wq_audio(jax.random.fold_in(key_list[10], 71), 0)
    wk_audio = draw_wk_audio(jax.random.fold_in(key_list[10], 71), 0)
    wv_audio = centred(key_list[9], (D, HEADS * HD), D ** -0.5, 0.109375, ((0, 128), (1, 2)))
    return dict(video=video, audio=audio, video_gain=video_gain, audio_gain=audio_gain, wq_video=wq_video, wk_video=wk_video, wv_video=wv_video, wq_audio=wq_audio, wk_audio=wk_audio, wv_audio=wv_audio)


def rms_norm(states, gain):
    values = states.astype(jnp.float32)
    inverse = lax.rsqrt(lax.optimization_barrier(jnp.mean(values * values, axis=-1, keepdims=True)) + 1e-06)
    return (values * inverse * gain).astype(jnp.bfloat16)

def project(states, weight):
    return jnp.dot(states, weight, preferred_element_type=jnp.float32).astype(jnp.bfloat16)

def reference(video, audio, video_gain, audio_gain, wq_video, wk_video, wv_video, wq_audio, wk_audio, wv_audio):
    scaling = HD ** (-0.5)
    normed_video = rms_norm(video, video_gain)
    normed_audio = rms_norm(audio, audio_gain)
    k_audio = project(normed_audio, wk_video).reshape(NA, HEADS, HD).astype(jnp.float32)
    v_audio = project(normed_audio, wv_video).reshape(NA, HEADS, HD).astype(jnp.float32)
    q_audio = project(normed_audio, wq_audio)
    k_video = project(normed_video, wk_audio)
    v_video = project(normed_video, wv_audio)

    def video_block(row_block):
        query = project(row_block, wq_video).reshape(TOK_DEV, HEADS, HD).astype(jnp.float32)
        scores = jnp.einsum('thd,ahd->hta', query, k_audio) * scaling
        top = lax.optimization_barrier(jnp.max(scores, axis=-1, keepdims=True))
        expo = jnp.exp(scores - top)
        totals = lax.optimization_barrier(jnp.sum(expo, axis=-1))
        weights = expo.astype(jnp.bfloat16).astype(jnp.float32)
        mixed = jnp.einsum('hta,ahd->thd', weights, v_audio) / jnp.transpose(totals)[:, :, None]
        return mixed.astype(jnp.bfloat16).reshape(TOK_DEV, HEADS * HD)
    video_mix = lax.map(video_block, normed_video.reshape(N_SEQ, TOK_DEV, D)).reshape(NV, HEADS * HD)

    def audio_head(items):
        query, keys, values = items
        scores = jnp.dot(query, keys.T, preferred_element_type=jnp.float32) * scaling
        top = lax.optimization_barrier(jnp.max(scores, axis=-1, keepdims=True))
        expo = jnp.exp(scores - top)
        totals = lax.optimization_barrier(jnp.sum(expo, axis=-1, keepdims=True))
        mixed = jnp.dot(expo.astype(jnp.bfloat16), values, preferred_element_type=jnp.float32) / totals
        return mixed.astype(jnp.bfloat16)
    query_heads = jnp.transpose(q_audio.reshape(NA, HEADS, HD), (1, 0, 2))
    key_heads = jnp.transpose(k_video.reshape(NV, HEADS, HD), (1, 0, 2))
    value_heads = jnp.transpose(v_video.reshape(NV, HEADS, HD), (1, 0, 2))
    audio_heads = lax.map(audio_head, (query_heads, key_heads, value_heads))
    audio_mix = jnp.transpose(audio_heads, (1, 0, 2)).reshape(NA, HEADS * HD)
    return (video_mix, audio_mix)
```

```python
import functools
import jax
import jax.numpy as jnp
from jax import lax
from jax.experimental import pallas as pl
from jax.experimental.pallas import tpu as pltpu
from jax.sharding import Mesh, PartitionSpec as P

D = 3072
HD = 128
SEQ = ("y", "x", "zh", "core")
Y, X, ZH, CORE = range(4)
RING = 4
HEADS_CORE = 3
WIDTH = HEADS_CORE * HD
STATS = WIDTH + HD
SUMS = 3 * WIDTH + HD
BLOCK = 80
F32 = jnp.float32
BF16 = jnp.bfloat16
join = lax.optimization_barrier


def shape(dims, dtype):
    return jax.ShapeDtypeStruct(dims, dtype)


def whole(a):
    return pl.BlockSpec(a.shape, lambda i, n=len(a.shape): (0,) * n)


def call(kernel, at, operands, outs, flops=0, scratch=(), specs=None, vmem=48):
    moved = sum(a.size * a.dtype.itemsize for a in operands)
    specs = specs or [whole(a) for a in operands]
    moved += sum(o.size * o.dtype.itemsize for o in outs)
    return pl.pallas_call(
        kernel,
        grid=(1,),
        out_shape=tuple(outs),
        in_specs=[pl.BlockSpec(memory_space=pltpu.SMEM)] + specs,
        out_specs=tuple(whole(o) for o in outs),
        scratch_shapes=list(scratch),
        compiler_params=pltpu.CompilerParams(vmem_limit_bytes=vmem * 1024 * 1024),
        cost_estimate=pl.CostEstimate(flops=flops, bytes_accessed=moved, transcendentals=0),
    )(at, *operands)


def dot(a, b):
    return jnp.dot(a, b, preferred_element_type=F32)


def dot_t(a, b):
    return lax.dot_general(a, b, (((1,), (1,)), ((), ())), preferred_element_type=F32)


def shifted(part, axis, by):
    size = lax.axis_size(axis)
    return lax.ppermute(part, axis, [(i, (i + by) % size) for i in range(size)])


def swapped(part, axis, bits):
    return lax.ppermute(part, axis, [(i, i ^ bits) for i in range(lax.axis_size(axis))])


def around(part, axis):
    return [part] + [swapped(part, axis, j) for j in range(1, RING)]


def handed_out(chunks, axis):
    return [chunks[0]] + [swapped(chunks[j], axis, j) for j in range(1, RING)]


def neighbours(part, axis):
    return [shifted(part, axis, -1), shifted(part, axis, 1)]


def beyond(near, axis):
    after, before = near
    half = after.shape[0] // 2
    return [shifted(before[:half], axis, 1), shifted(after[half:], axis, -1)]


ORDER = (1, 2, 0, 3, 4, 5)


def prepare_kernel(at, *refs):
    weights, (audio, gain), (own, other, payload) = refs[:6], refs[6:8], refs[8:]
    is_first = at[CORE] == 0
    for place, i in enumerate(ORDER):
        cut = slice(place * WIDTH, (place + 1) * WIDTH)
        lower, upper = weights[i][:, :WIDTH], weights[i][:, WIDTH:]
        own[:, cut] = jnp.where(is_first, lower, upper)
        other[:, cut] = jnp.where(is_first, upper, lower)
    values = audio[...].astype(F32)
    squares = jnp.sum(values * values, axis=1, keepdims=True)
    rows, used = values.shape
    payload[...] = jnp.concatenate(
        [values * gain[...], squares, jnp.zeros((rows, HD - used - 1), F32)], axis=1
    )


def front_kernel(used, at, w_own, w_other, p_own, p_other, pair, o0, o1, o2, o3, held):
    is_first = at[CORE] == 0
    video = 3 * WIDTH
    mine, theirs = w_own[:, :video].astype(F32), w_other[:, :video].astype(F32)
    pair[...] = jnp.concatenate(
        [jnp.where(is_first, mine, theirs), jnp.where(is_first, theirs, mine)], axis=0
    ).astype(BF16)
    sums = dot(p_own[:, :used].astype(BF16), w_own[:, video:]) + dot(
        p_other[:, :used].astype(BF16), w_other[:, video:]
    )
    squares = p_own[:, used : used + 1] + p_other[:, used : used + 1]
    sums = jnp.concatenate([sums, jnp.broadcast_to(squares, (sums.shape[0], HD))], axis=1)
    small = sums.shape[0] // (RING * RING)
    for s in range(RING):
        held[s] = jnp.concatenate(
            [sums[(t * RING + s) * small : (t * RING + s + 1) * small] for t in range(RING)], axis=0
        )
    for j, out in enumerate((o0, o1, o2, o3)):
        out[...] = held[at[X] ^ j].astype(BF16)


def sum_kernel(at, c0, c1, c2, c3, o0, o1, o2, o3, held):
    sums = (c0[...].astype(F32) + c1[...].astype(F32)) + (c2[...].astype(F32) + c3[...].astype(F32))
    pair = sums.shape[0] // (RING * RING)
    for s in range(RING):
        held[s] = jnp.concatenate(
            [sums[(t * RING + s) * pair : (t * RING + s + 1) * pair] for t in range(RING)], axis=0
        )
    for j, out in enumerate((o0, o1, o2, o3)):
        out[...] = held[at[ZH] ^ j]


def place_kernel(axis_at, cuts, at, *refs):
    pieces, outs = refs[:RING], refs[RING:]
    for j, piece in enumerate(pieces):
        for out, (first, last) in zip(outs, cuts):
            out[at[axis_at] ^ j] = piece[:, first:last]


def place(at, axis_at, pieces, cuts):
    rows = pieces[0].shape[0]
    outs = [shape((RING, rows, last - first), BF16) for first, last in cuts]
    placed = call(functools.partial(place_kernel, axis_at, cuts), at, pieces, outs)
    return [p.reshape(RING * rows, p.shape[-1]) for p in placed]


def place_ring_kernel(axis_at, cuts, at, own, after, before, top, bottom, *outs):
    half = top.shape[0]
    for out, (first, last) in zip(outs, cuts):
        cut = slice(first, last)
        out[at[axis_at]] = own[:, cut]
        out[lax.rem(at[axis_at] + 1, RING)] = after[:, cut]
        out[lax.rem(at[axis_at] + 3, RING)] = before[:, cut]
        far = lax.rem(at[axis_at] + 2, RING)
        out[far, :half] = top[:, cut]
        out[far, half:] = bottom[:, cut]


def place_ring(at, axis_at, pieces, cuts):
    rows = pieces[0].shape[0]
    outs = [shape((RING, rows, last - first), BF16) for first, last in cuts]
    placed = call(functools.partial(place_ring_kernel, axis_at, cuts), at, pieces, outs)
    return [p.reshape(RING * rows, p.shape[-1]) for p in placed]


def tokens_kernel(at, own, other, gain, by_y, by_x):
    rows = own.shape[0]
    wide = D // RING
    narrow = wide // RING
    for source, base in ((own, 0), (other, rows)):
        for first in range(0, rows, BLOCK):
            values = source[first : first + BLOCK, :].astype(F32)
            inverse = lax.rsqrt(jnp.mean(values * values, axis=1, keepdims=True) + 1e-06)
            normed = (values * inverse * gain[...]).astype(BF16)
            to = slice(base + first, base + first + BLOCK)
            for s in range(RING):
                slot_y = lax.rem(s - at[Y] + RING, RING)
                slot_x = lax.rem(s - at[X] + RING, RING)
                by_y[slot_y, to, :] = normed[:, s * wide : (s + 1) * wide]
                strips = [
                    normed[:, t * wide + s * narrow : t * wide + (s + 1) * narrow]
                    for t in range(RING)
                ]
                by_x[slot_x, to, :] = jnp.concatenate(strips, axis=1)


def near_kernel(at, by_y, by_x, k0, k1, k3, v0, v1, v3, k_sum, v_sum):
    k_sum[...] = dot(by_x[0], k0[...]) + dot(by_x[1], k1[...]) + dot(by_x[3], k3[...])
    v_sum[...] = dot(by_y[0], v0[...]) + dot(by_y[1], v1[...]) + dot(by_y[3], v3[...])


def far_kernel(at, far_y, far_x, k_top, k_bottom, v_top, v_bottom, k_sum, v_sum, keys, values):
    half = k_top.shape[0]
    far = far_x[0]
    keys[...] = (
        k_sum[...] + dot(far[:, :half], k_top[...]) + dot(far[:, half:], k_bottom[...])
    ).astype(BF16)
    far = far_y[0]
    values[...] = (
        v_sum[...] + dot(far[:, :half], v_top[...]) + dot(far[:, half:], v_bottom[...])
    ).astype(BF16)


def audio_kernel(at, keys, values, a0, a1, a2, a3, *outs):
    queries = jnp.concatenate([a[:, :WIDTH] for a in (a0, a1, a2, a3)], axis=0)
    lane = lax.broadcasted_iota(jnp.int32, (queries.shape[0], HD), 1)
    stats = jnp.zeros((queries.shape[0], HD), F32)
    rows = a0.shape[0]
    for h in range(HEADS_CORE):
        cut = slice(h * HD, (h + 1) * HD)
        scores = dot_t(queries[:, cut], keys[:, cut]) * (HD**-0.5)
        top = jnp.max(scores, axis=1, keepdims=True)
        expo = jnp.exp(scores - top)
        total = jnp.sum(expo, axis=1, keepdims=True)
        acc = dot(expo.astype(BF16), values[:, cut])
        stats = jnp.where(lane == h, top, stats)
        stats = jnp.where(lane == HEADS_CORE + h, total, stats)
        for j, out in enumerate(outs):
            out[:, cut] = acc[j * rows : (j + 1) * rows]
    for j, out in enumerate(outs):
        out[:, WIDTH:] = stats[j * rows : (j + 1) * rows]


def merged(parts):
    heads = []
    for h in range(HEADS_CORE):
        tops = [p[:, WIDTH + h : WIDTH + h + 1] for p in parts]
        totals = [p[:, WIDTH + HEADS_CORE + h : WIDTH + HEADS_CORE + h + 1] for p in parts]
        accs = [p[:, h * HD : (h + 1) * HD] for p in parts]
        top = jnp.maximum(jnp.maximum(tops[0], tops[1]), jnp.maximum(tops[2], tops[3]))
        factors = [jnp.exp(t - top) for t in tops]
        total = sum(t * f for t, f in zip(totals, factors))
        acc = sum(a * f for a, f in zip(accs, factors))
        heads.append((top, total, acc))
    return heads


def state_of(heads):
    rows = heads[0][0].shape[0]
    lane = lax.broadcasted_iota(jnp.int32, (rows, HD), 1)
    stats = jnp.zeros((rows, HD), F32)
    for h, (top, total, _) in enumerate(heads):
        stats = jnp.where(lane == h, top, stats)
        stats = jnp.where(lane == HEADS_CORE + h, total, stats)
    return jnp.concatenate([acc for _, _, acc in heads] + [stats], axis=1)


def merge_x_kernel(at, p0, p1, p2, p3, *outs):
    state = state_of(merged([p0[...], p1[...], p2[...], p3[...]]))
    rows = outs[0].shape[0]
    for j, out in enumerate(outs):
        out[...] = state[j * rows : (j + 1) * rows]


def merge_z_kernel(at, p0, p1, p2, p3, o0, o1, o2, o3, held):
    state = state_of(merged([p0[...], p1[...], p2[...], p3[...]]))
    rows = o0.shape[0]
    for j in range(RING):
        held[j] = state[j * rows : (j + 1) * rows]
    for j, out in enumerate((o0, o1, o2, o3)):
        out[...] = held[at[Y] ^ j]


def merge_y_kernel(at, p0, p1, p2, p3, own, other):
    heads = merged([p0[...], p1[...], p2[...], p3[...]])
    mixed = jnp.concatenate([acc / total for _, total, acc in heads], axis=1)
    is_first = at[CORE] == 0
    own[...] = jnp.where(is_first, mixed[:1], mixed[1:]).astype(BF16)
    other[...] = jnp.where(is_first, mixed[1:], mixed[:1]).astype(BF16)


def video_kernel(at, by_y, q0, q1, q3, q_top, q_bottom, a0, a1, a2, a3, out_own, out_other):
    audio = jnp.concatenate([a[...] for a in (a0, a1, a2, a3)], axis=0)
    half = q_top.shape[0]
    far = by_y[2]
    queries = (
        dot(by_y[0], q0[...])
        + dot(by_y[1], q1[...])
        + dot(by_y[3], q3[...])
        + dot(far[:, :half], q_top[...])
        + dot(far[:, half:], q_bottom[...])
    ).astype(BF16)
    rows = out_own.shape[0]
    for h in range(HEADS_CORE):
        cut = slice(h * HD, (h + 1) * HD)
        keys = audio[:, WIDTH + h * HD : WIDTH + (h + 1) * HD]
        values = audio[:, 2 * WIDTH + h * HD : 2 * WIDTH + (h + 1) * HD]
        scores = dot_t(queries[:, cut], keys) * (HD**-0.5)
        top = jnp.max(scores, axis=1, keepdims=True)
        expo = jnp.exp(scores - top)
        total = jnp.sum(expo, axis=1, keepdims=True)
        mixed = (dot(expo.astype(BF16), values) / total).astype(BF16)
        out_own[:, cut] = mixed[:rows]
        out_other[:, cut] = mixed[rows:]


def shards(
    video, audio, video_gain, audio_gain, wq_video, wk_video, wv_video, wq_audio, wk_audio, wv_audio
):
    at = jnp.stack([lax.axis_index(a) for a in SEQ]).astype(jnp.int32)
    first = at[CORE] == 0
    tok, used = video.shape[0], audio.shape[1]
    na = audio.shape[0]
    group, small, pair_rows = na // RING, na // RING**2, na // RING**3
    mac = 2 * 2 * tok * WIDTH * D // RING
    key_cut, value_cut, query_cut = [(i * WIDTH, (i + 1) * WIDTH) for i in range(3)]

    video_other = shifted(video, "core", 1)
    w_own, w_other, payload = call(
        prepare_kernel,
        at,
        [wq_video, wk_audio, wv_audio, wq_audio, wk_video, wv_video, audio, audio_gain[None, :]],
        [shape((wq_video.shape[0], 6 * WIDTH), BF16)] * 2 + [shape((na, HD), F32)],
        vmem=60,
    )
    w_other, payload_other = shifted(w_other, "core", 1), shifted(payload, "core", 1)
    pair, *sums = call(
        functools.partial(front_kernel, used),
        at,
        [w_own, w_other, payload, payload_other],
        [shape((2 * wq_video.shape[0], 3 * WIDTH), BF16)] + [shape((group, SUMS), BF16)] * RING,
        scratch=[pltpu.VMEM((RING, group, SUMS), F32)],
    )
    video_other, pair, sums = join((video_other, pair, sums))

    weights = around(pair, "zh")
    sums = handed_out(sums, "x")
    by_y, by_x = call(
        tokens_kernel,
        at,
        [video, video_other, video_gain[None, :]],
        [shape((RING, 2 * tok, D // RING), BF16)] * 2,
    )
    weights, sums, by_y, by_x = join((weights, sums, by_y, by_x))

    k_z, vq_z = place(at, ZH, weights, (key_cut, (WIDTH, 3 * WIDTH)))
    k_y, vq_near = around(k_z, "y"), neighbours(vq_z, "x")
    sums = call(
        sum_kernel,
        at,
        sums,
        [shape((small, SUMS), F32)] * RING,
        scratch=[pltpu.VMEM((RING, small, SUMS), F32)],
    )
    k_y, vq_near, sums = join((k_y, vq_near, sums))
    vq_far = beyond(vq_near, "x")
    sums = handed_out(sums, "zh")
    (k_y,) = place(at, Y, k_y, ((0, WIDTH),))
    k_y, vq_far, sums = join((k_y, vq_far, sums))

    v_x, q_x = place_ring(at, X, [vq_z, *vq_near, *vq_far], ((0, WIDTH), (WIDTH, 2 * WIDTH)))
    k_near, v_near = neighbours(k_y, "x"), neighbours(v_x, "y")
    sums = (sums[0] + sums[1]) + (sums[2] + sums[3])
    sums = sums + swapped(sums, "y", 1)
    sums = sums + swapped(sums, "y", 2)
    k_near, v_near, sums = join((k_near, v_near, sums))

    k_far, v_far = beyond(k_near, "x"), beyond(v_near, "y")
    inverse = lax.rsqrt(sums[:, 3 * WIDTH : 3 * WIDTH + 1] / D + 1e-06)
    projected = (sums[:, : 3 * WIDTH] * inverse).astype(BF16)
    projected = jnp.concatenate([projected, swapped(projected, "zh", 1)], axis=0)
    projected = jnp.concatenate([projected, swapped(projected, "zh", 2)], axis=0)
    k_sum, v_sum = call(
        near_kernel,
        at,
        [by_y, by_x, k_y, *k_near, v_x, *v_near],
        [shape((2 * tok, WIDTH), F32)] * 2,
        flops=6 * mac,
    )
    k_far, v_far, projected, k_sum, v_sum, q_x = join(
        (k_far, v_far, projected, k_sum, v_sum, q_x)
    )

    audio_all = around(projected, "x")
    q_near = neighbours(q_x, "y")
    keys, values = call(
        far_kernel,
        at,
        [by_y, by_x, *k_far, *v_far, k_sum, v_sum],
        [shape((2 * tok, WIDTH), BF16)] * 2,
        flops=2 * mac,
        specs=[pl.BlockSpec((1,) + by_y.shape[1:], lambda i: (2, 0, 0))] * 2
        + [whole(a) for a in (*k_far, *v_far, k_sum, v_sum)],
    )
    states = call(
        audio_kernel,
        at,
        [keys, values, *audio_all],
        [shape((group, STATS), F32)] * RING,
        flops=mac // 2,
    )
    q_near, states = join((q_near, states))

    states = handed_out(states, "x")
    q_far = beyond(q_near, "y")
    states = call(merge_x_kernel, at, states, [shape((small, STATS), F32)] * RING)
    states = handed_out(states, "zh")
    states = call(
        merge_z_kernel,
        at,
        states,
        [shape((pair_rows, STATS), F32)] * RING,
        scratch=[pltpu.VMEM((RING, pair_rows, STATS), F32)],
    )
    states, q_far = join((states, q_far))
    mixed_own, mixed_other = call(
        merge_y_kernel, at, handed_out(states, "y"), [shape((1, WIDTH), BF16)] * 2
    )
    mixed_other = shifted(mixed_other, "core", 1)
    audio_mix = jnp.where(
        first,
        jnp.concatenate([mixed_own, mixed_other], axis=1),
        jnp.concatenate([mixed_other, mixed_own], axis=1),
    )

    out_own, out_other = call(
        video_kernel,
        at,
        [by_y, q_x, *q_near, *q_far, *audio_all],
        [shape((tok, WIDTH), BF16)] * 2,
        flops=4 * mac,
    )
    out_other = shifted(out_other, "core", 1)
    video_mix = jnp.where(
        first,
        jnp.concatenate([out_own, out_other], axis=1),
        jnp.concatenate([out_other, out_own], axis=1),
    )
    return (video_mix, audio_mix)


def solution(mesh):
    fine = Mesh(mesh.devices.reshape(RING, RING, RING, 2, 2), SEQ + ("head",))
    weight = P(SEQ, "head")
    in_specs = (P(SEQ, None), P(None, SEQ), P(), P(SEQ)) + (weight,) * 6
    out_specs = (weight, weight)
    return jax.shard_map(shards, mesh=fine, in_specs=in_specs, out_specs=out_specs, check_vma=False)
```
